32 devices in a mesh: seq: 16 (over z, y, core), tp: 2 (over x).
Axes of the slice: x: 2, y: 2, z: 4, core: 2. Of those that a mesh axis runs over, the one named last changes fastest.
Arguments:
- query_proj: bfloat16 [4096, 3072], P('seq', 'tp'), may hold values from -8 to 8
- key_proj: bfloat16 [4096, 3072], P('seq', 'tp'), may hold values from -8 to 8
- value_proj: bfloat16 [4096, 3072], P('seq', 'tp'), may hold values from -6 to 6
- hidden: bfloat16 [4096, 3072], P('seq', 'tp'), may hold values from -2 to 2
- out_weight: bfloat16 [3072, 3072], P('tp'), may hold values from -0.109375 to 0.109375
- norm_gain: bfloat16 [3072], P('tp'), may hold values from 0.099609375 to 1.8984375
- segment_ids: int32 [4096], P('seq'), may hold values from 0 to 7, never falling along the last dimension, each value on 1 to 2048 neighbouring positions
- pad_mask: int32 [4096], P('seq'), may hold values 0 or 1
- page_table: int32 [32], P('seq'), may hold values from 0 to 1, as said below
Outputs:
- hidden_out: bfloat16 [4096, 3072], P('seq', 'tp')
- normed: bfloat16 [4096, 3072], P('seq', 'tp')
- kv_pages: bfloat16 [32, 2, 128, 3072], P('seq', None, None, 'tp')
The draws below stay inside these ranges and needn't reach their ends.
Inputs may be any that keep to these rules, and one draw needn't show every extreme that they name: `segment_ids`: never falling along the tokens; each of the 8 prompts has 1 to 2048 tokens, one exactly 2048. `page_table`: the 2 pages of each aligned block of 2 pages name each slot once.
All inputs are finite; a program needn't handle non-finite values. No bound on the sum of `pad_mask` on one device may be relied on, other than what follows from the above.
Results may differ from the reference program's by a relative error of at most 0.014.
Values may be sent and summed in bfloat16 or wider, within the bound.
A program may use at most 128 MiB of HBM per device.

```python
import math
import jax
import jax.numpy as jnp
import numpy as np
from jax import lax

D = 3072
HEADS = 32
HEAD_DIM = 96
TOK_DEV = 256
PAGE = 128
TOKENS = 4096
SEG_MOST = 2048
SEGS = 8
PAGES = 32
PAGES_DEV = 2


def query_and_key(key):
    base = jax.random.fold_in(key, 11)
    key_query, key_keys = jax.random.split(base, 2)
    width_all = HEADS * HEAD_DIM
    q_values = jnp.clip(jax.random.normal(key_query, (TOKENS, width_all), jnp.float32), -6.0, 6.0)
    k_values = jnp.clip(jax.random.normal(key_keys, (TOKENS, width_all), jnp.float32), -6.0, 6.0)
    return (q_values, k_values)


def draw_query_proj(key, part):
    return query_and_key(key)[0].astype(jnp.bfloat16)


def draw_key_proj(key, part):
    return query_and_key(key)[1].astype(jnp.bfloat16)


def draw_hidden(key, part):
    key_main, key_rows, key_cols = jax.random.split(jax.random.fold_in(key, 23), 3)
    column = jnp.arange(D).astype(jnp.float32) / D
    base_values = jnp.clip(jax.random.normal(key_main, (TOKENS, D), jnp.float32), -6.0, 6.0)
    rising = jnp.exp(jnp.log(3.0) * column)
    row_scale = jnp.exp(jnp.log(10.0) * jax.random.uniform(key_rows, (TOKENS,), jnp.float32))
    col_scale = jnp.exp(jnp.log(10.0) * jax.random.uniform(key_cols, (D,), jnp.float32)) * rising
    result = 0.005 * base_values * row_scale[:, None] * col_scale[None, :]
    return jnp.clip(result, -2.0, 2.0).astype(jnp.bfloat16)


def draw_page_table(key, part):
    scores = jax.random.randint(jax.random.fold_in(key, 31), (PAGES // PAGES_DEV, PAGES_DEV), 0, 1048576)
    scores = scores * PAGES_DEV + jnp.arange(PAGES_DEV, dtype=jnp.int32)[None, :]
    return jnp.argsort(scores, axis=1).astype(jnp.int32).reshape(PAGES)


def with_ends(entries, own_key, low, top_value):
    dims = entries.shape
    place = [jax.random.randint(jax.random.fold_in(own_key, axis), (), 0, dims[axis]) for axis in range(len(dims))]
    entries = entries.at[tuple(place)].set(low)
    longest = dims.index(max(dims))
    place[longest] = (place[longest] + 1) % dims[longest]
    return entries.at[tuple(place)].set(top_value)


def levels(key, extent, cuts, least, top_value):
    factor_of = 1.0
    for axis_at, blocks in cuts:
        draws = jax.random.uniform(jax.random.fold_in(jax.random.fold_in(key, 6), axis_at), (blocks,), jnp.float32, least / len(cuts), top_value / len(cuts))
        factor_of = factor_of * jnp.repeat(jnp.exp(draws), extent[axis_at] // blocks).reshape((-1,) + (1,) * (len(extent) - 1 - axis_at))
    return factor_of


def length_profile(count, total, bound, lean):
    portions = [(1 << 20) // math.isqrt(standing ** lean) + 1 for standing in range(2, count + 1)]
    rest, given = total - bound - (count - 1), [1] * (count - 1)
    while rest > 0:
        free = [i for i in range(count - 1) if given[i] < bound]
        pool, budget = sum([portions[i] for i in free]), rest
        for i in free:
            addition = min(bound - given[i], max(1, budget * portions[i] // pool), rest)
            given[i] = given[i] + addition
            rest = rest - addition
    return np.array([bound] + given)


def ragged_sizes(own_key, number_of, total, limit, lean):
    if number_of == 2:
        one = jax.random.randint(own_key, (), max(1, total - limit), min(limit, total - 1) + 1)
        return jnp.stack([one, total - one])
    sizes = jnp.asarray(length_profile(number_of, total, limit, lean), jnp.int32)
    twos = (number_of - 1) // 2
    giver, taker = sizes[1:1 + 2 * twos:2], sizes[2:2 + 2 * twos:2]
    room = jnp.minimum(giver - 1, limit - taker)
    moved = jax.random.randint(jax.random.fold_in(own_key, 1), (twos,), 0, 1 << 20) % (room + 1)
    sizes = sizes.at[1:1 + 2 * twos:2].set(giver - moved).at[2:2 + 2 * twos:2].set(taker + moved)
    return sizes[jax.random.permutation(jax.random.fold_in(own_key, 2), number_of)]


def noise(rng, dims, width, limit, pieces=(), kind=jnp.bfloat16):
    entries = jax.random.normal(rng, dims, jnp.float32) * width
    if len(pieces) > 0:
        entries = levels(rng, dims, pieces, -0.22, 0.18) * entries
    return jnp.clip(entries, min=-limit, max=limit).astype(kind)


def setup_inputs(seed: int = 0) -> dict:
    key_list = jax.random.split(jax.random.key(seed), 10)
    query_proj = draw_query_proj(jax.random.fold_in(key_list[9], 71), 0)
    key_proj = draw_key_proj(jax.random.fold_in(key_list[9], 71), 0)
    value_proj = noise(key_list[2], (TOKENS, HEADS * HEAD_DIM), 1.0, 6.0, ((0, 16), (1, 2)))
    hidden = draw_hidden(jax.random.fold_in(key_list[9], 71), 0)
    out_weight = noise(key_list[4], (HEADS * HEAD_DIM, D), (HEADS * HEAD_DIM) ** -0.5, 0.109375, ((0, 2),))
    norm_gain = jnp.clip(1.0 + 0.18 * jax.random.normal(key_list[5], (D,), jnp.float32), 0.099609375, 1.8984375).astype(jnp.bfloat16)
    segment_ids = jnp.searchsorted(jnp.cumsum(ragged_sizes(key_list[6], SEGS, TOKENS, SEG_MOST, 2)), jnp.arange(TOKENS), side="right").astype(jnp.int32)
    pad_mask = with_ends((jax.random.randint(key_list[7], (TOKENS,), 0, 8) < 7).astype(jnp.int32), jax.random.fold_in(key_list[7], 1), 0, 1)
    page_table = draw_page_table(jax.random.fold_in(key_list[9], 71), 0)
    return dict(query_proj=query_proj, key_proj=key_proj, value_proj=value_proj, hidden=hidden, out_weight=out_weight, norm_gain=norm_gain, segment_ids=segment_ids, pad_mask=pad_mask, page_table=page_table)


far_index = 1073741824
masked_score = -1e+30
norm_epsilon = 1e-05

def rotate(values_in, position, head_count, head_dim):
    count_rows = values_in.shape[0]
    half_dim = head_dim // 2
    frequency = jnp.exp(jnp.arange(half_dim, dtype=jnp.float32) * (-2.0 * math.log(10000.0) / head_dim))
    angles = position.astype(jnp.float32)[:, None] * frequency[None, :]
    cosine = jnp.cos(angles)[:, None, :]
    sine_part = jnp.sin(angles)[:, None, :]
    as_float = values_in.astype(jnp.float32).reshape(count_rows, head_count, head_dim)
    lower_half = as_float[..., :half_dim]
    upper_half = as_float[..., half_dim:]
    rotated = jnp.concatenate([lower_half * cosine - upper_half * sine_part, upper_half * cosine + lower_half * sine_part], axis=-1)
    return rotated.reshape(count_rows, head_count * head_dim).astype(jnp.bfloat16)

def reference(query_proj, key_proj, value_proj, hidden, out_weight, norm_gain, segment_ids, pad_mask, page_table):
    tok_index = jnp.arange(TOKENS, dtype=jnp.int32)
    member = segment_ids[:, None] == jnp.arange(SEGS, dtype=jnp.int32)[None, :]
    seg_start = lax.optimization_barrier(jnp.min(jnp.where(member, tok_index[:, None], far_index), axis=0))
    position = tok_index - lax.optimization_barrier(jnp.sum(jnp.where(member, seg_start[None, :], 0), axis=1))
    q_rot = rotate(query_proj, position, HEADS, HEAD_DIM)
    k_rot = rotate(key_proj, position, HEADS, HEAD_DIM)
    key_tag = jnp.where(pad_mask == 1, segment_ids + 1, 0)
    key_window = min(SEG_MOST + TOK_DEV, TOKENS)
    factor = 1.0 / math.sqrt(HEAD_DIM)

    def one_block(block_index):
        q_start = (block_index * TOK_DEV).astype(jnp.int32)
        k_start = jnp.clip(q_start + TOK_DEV - key_window, 0, TOKENS - key_window).astype(jnp.int32)
        query_heads = lax.dynamic_slice_in_dim(q_rot, q_start, TOK_DEV, 0).astype(jnp.float32).reshape(TOK_DEV, HEADS, HEAD_DIM)
        key_heads = lax.dynamic_slice_in_dim(k_rot, k_start, key_window, 0).astype(jnp.float32).reshape(key_window, HEADS, HEAD_DIM)
        val_heads = lax.dynamic_slice_in_dim(value_proj, k_start, key_window, 0).astype(jnp.float32).reshape(key_window, HEADS, HEAD_DIM)
        query_seg = lax.dynamic_slice_in_dim(segment_ids, q_start, TOK_DEV, 0)
        tags = lax.dynamic_slice_in_dim(key_tag, k_start, key_window, 0)
        query_pos = q_start + jnp.arange(TOK_DEV, dtype=jnp.int32)
        key_pos = k_start + jnp.arange(key_window, dtype=jnp.int32)
        visible = (tags[None, :] == query_seg[:, None] + 1) & (key_pos[None, :] <= query_pos[:, None]) | (key_pos[None, :] == query_pos[:, None])
        logits = jnp.einsum('qhd,khd->hqk', query_heads, key_heads) * factor
        logits = jnp.where(visible[None], logits, masked_score)
        row_peak = lax.optimization_barrier(jnp.max(logits, axis=-1, keepdims=True))
        unnormed = jnp.where(visible[None], jnp.exp(logits - row_peak), 0.0)
        denom = lax.optimization_barrier(jnp.sum(unnormed, axis=-1))
        weights = unnormed.astype(jnp.bfloat16)
        weighted = jnp.einsum('hqk,khd->qhd', weights.astype(jnp.float32), val_heads)
        result = weighted / jnp.transpose(denom)[:, :, None]
        return result.reshape(TOK_DEV, HEADS * HEAD_DIM).astype(jnp.bfloat16)
    attn = lax.map(one_block, jnp.arange(TOKENS // TOK_DEV, dtype=jnp.int32)).reshape(TOKENS, HEADS * HEAD_DIM)
    proj = jnp.dot(attn, out_weight, preferred_element_type=jnp.float32)
    hidden_out = (hidden.astype(jnp.float32) + proj).astype(jnp.bfloat16)
    stream_wide = hidden_out.astype(jnp.float32)
    mean_square = lax.optimization_barrier(jnp.mean(stream_wide * stream_wide, axis=1, keepdims=True))
    normed = (stream_wide * lax.rsqrt(mean_square + norm_epsilon) * norm_gain.astype(jnp.float32)[None, :]).astype(jnp.bfloat16)
    pad_scale = pad_mask.astype(jnp.bfloat16)[:, None]
    stacked = jnp.stack([k_rot * pad_scale, value_proj * pad_scale])
    stacked = stacked.reshape(2, PAGES, PAGE, HEADS * HEAD_DIM).transpose(1, 0, 2, 3)
    destination = jnp.arange(PAGES, dtype=jnp.int32) // PAGES_DEV * PAGES_DEV + page_table
    kv_pages = jnp.zeros_like(stacked).at[destination].set(stacked)
    return (hidden_out, normed, kv_pages)
```

```python
import functools
import math

import jax
import jax.numpy as jnp
from jax import lax
from jax.experimental import pallas as pl
from jax.experimental.pallas import tpu as pltpu
from jax.sharding import PartitionSpec as P

D = 3072
HEAD_DIM = 96
HALF = HEAD_DIM // 2
PAGE = 128
LEVEL = 4
CHUNKS = 4
COLS = 384

far_index = 1073741824
masked_score = -1e30
norm_epsilon = 1e-05
MESH = pl.DeviceIdType.MESH


def rotate(values_in, position, head_count, head_dim):
    count_rows = values_in.shape[0]
    half_dim = head_dim // 2
    frequency = jnp.exp(
        jnp.arange(half_dim, dtype=jnp.float32) * (-2.0 * math.log(10000.0) / head_dim)
    )
    angles = position.astype(jnp.float32)[:, None] * frequency[None, :]
    cosine = jnp.cos(angles)[:, None, :]
    sine_part = jnp.sin(angles)[:, None, :]
    as_float = values_in.astype(jnp.float32).reshape(count_rows, head_count, head_dim)
    lower_half = as_float[..., :half_dim]
    upper_half = as_float[..., half_dim:]
    rotated = jnp.concatenate(
        [
            lower_half * cosine - upper_half * sine_part,
            upper_half * cosine + lower_half * sine_part,
        ],
        axis=-1,
    )
    return rotated.reshape(count_rows, head_count * head_dim).astype(jnp.bfloat16)


def kernel(
    seq,
    tp,
    q_ref,
    k_ref,
    v_ref,
    hid_ref,
    gain_ref,
    cos_ref,
    sin_ref,
    kaug_ref,
    qaug_ref,
    bias_ref,
    w_hbm,
    out_ref,
    norm_ref,
    kv,
    qx,
    flip,
    attn,
    m_s,
    l_s,
    acc,
    w_s,
    own_p,
    sbuf,
    rbuf,
    ssq_s,
    ssq_r,
    w_sem,
    z_send,
    y_send,
    c_send,
    d_send,
    recv,
    p_send,
    p_recv,
    s_send,
    s_recv,
):
    tok, feat = q_ref.shape
    heads = feat // HEAD_DIM
    hc = heads // CHUNKS
    fc = hc * HEAD_DIM
    aug = kaug_ref.shape[0]
    reach = seq // (2 * LEVEL)
    nt = feat // COLS
    me = lax.axis_index("seq")
    me_tp = lax.axis_index("tp")
    z = me // LEVEL
    m = me % LEVEL
    my = m // 2
    mc = m % 2
    core_mem = my * 2 + (1 - mc)
    y_mem = (1 - my) * 2 + mc
    diag_mem = (1 - my) * 2 + (1 - mc)
    core_dev = z * LEVEL + core_mem
    y_dev = z * LEVEL + y_mem
    last_z = seq // LEVEL - 1

    w_copy = pltpu.make_async_copy(w_hbm, w_s, w_sem)
    w_copy.start()

    barrier = pltpu.get_barrier_semaphore()
    for dev in (core_dev, y_dev):
        pl.semaphore_signal(barrier, inc=1, device_id=(dev, me_tp), device_id_type=MESH)
    for j in range(1, tp):
        pl.semaphore_signal(
            barrier, inc=1, device_id=(me, (me_tp + j) % tp), device_id_type=MESH
        )

    @pl.when(z > 0)
    def _():
        pl.semaphore_signal(barrier, inc=1, device_id=(me - LEVEL, me_tp), device_id_type=MESH)

    @pl.when(z < last_z)
    def _():
        pl.semaphore_signal(barrier, inc=1, device_id=(me + LEVEL, me_tp), device_id_type=MESH)

    flip[...] = v_ref[...].T
    for ch in range(CHUNKS):
        kv[m, ch, pl.ds(fc, fc), :] = flip[pl.ds(ch * fc, fc), :]
        kv[m, ch, pl.ds(2 * fc, aug), :] = kaug_ref[...]
    flip[...] = k_ref[...].T
    cosine = cos_ref[...]
    sine = sin_ref[...]

    peers = 1 + tp + (z > 0).astype(jnp.int32) + (z < last_z).astype(jnp.int32)
    pl.semaphore_wait(barrier, peers)

    def move(src_slot, dst_slot, ch, sem, dev):
        return pltpu.make_async_remote_copy(
            src_ref=kv.at[src_slot, ch],
            dst_ref=kv.at[dst_slot, ch],
            send_sem=sem,
            recv_sem=recv.at[dst_slot, ch],
            device_id=(dev, me_tp),
            device_id_type=MESH,
        )

    def z_copy(lev, ch):
        return move(lev * LEVEL + m, (lev + 1) * LEVEL + m, ch, z_send.at[lev, ch], me + LEVEL)

    def y_copy(lev, ch):
        slot = lev * LEVEL + m
        return move(slot, slot, ch, y_send.at[lev, ch], y_dev)

    def c_copy(lev, ch):
        slot = lev * LEVEL + m
        return move(slot, slot, ch, c_send.at[lev, ch], core_dev)

    def d_copy(lev, ch):
        slot = lev * LEVEL + y_mem
        return move(slot, slot, ch, d_send.at[lev, ch], core_dev)

    def arrived(slot, ch):
        pltpu.make_async_remote_copy(
            src_ref=kv.at[slot, ch],
            dst_ref=kv.at[slot, ch],
            send_sem=z_send.at[0, 0],
            recv_sem=recv.at[slot, ch],
            device_id=(core_dev, me_tp),
            device_id_type=MESH,
        ).wait_recv()

    def z_on(lev):
        return (z - lev >= 0) & (z < last_z) & (lev < reach)

    def band(lev, src, dst):
        return (z - lev >= 0) & ((lev > 0) | (src <= dst)) & ((lev < reach) | (src >= dst))

    def y_on(lev):
        return band(lev, my, 1 - my)

    def b_on(lev):
        return band(lev, 1 - my, my)

    def c_on(lev):
        return band(lev, mc, 1 - mc)

    def cr_on(lev):
        return band(lev, 1 - mc, mc)

    def send_column(lev, ch):
        @pl.when(z_on(lev))
        def _():
            z_copy(lev, ch).start()

        @pl.when(y_on(lev))
        def _():
            y_copy(lev, ch).start()

        @pl.when(c_on(lev))
        def _():
            c_copy(lev, ch).start()

    def turned(x, scale):
        low = x[:HALF].astype(jnp.float32)
        high = x[HALF:].astype(jnp.float32)
        return (
            ((low * cosine - high * sine) * scale).astype(jnp.bfloat16),
            ((high * cosine + low * sine) * scale).astype(jnp.bfloat16),
        )

    for ch in range(CHUNKS):
        for hh in range(hc):
            first, second = turned(flip[pl.ds((ch * hc + hh) * HEAD_DIM, HEAD_DIM), :], 1.0)
            kv[m, ch, pl.ds(hh * HEAD_DIM, HALF), :] = first
            kv[m, ch, pl.ds(hh * HEAD_DIM + HALF, HALF), :] = second
        send_column(0, ch)

    flip[...] = q_ref[...].T
    for h in range(heads):
        first, second = turned(
            flip[pl.ds(h * HEAD_DIM, HEAD_DIM), :], math.log2(math.e) / math.sqrt(HEAD_DIM)
        )
        qx[h, pl.ds(0, HALF), :] = first
        qx[h, pl.ds(HALF, HALF), :] = second
        qx[h, pl.ds(HEAD_DIM, aug), :] = qaug_ref[...]

    cross = (((0,), (0,)), ((), ()))

    def own_chunk(ch, carry):
        for hh in range(hc):
            h = ch * hc + hh
            keys = kv[m, ch, pl.ds(hh * HEAD_DIM, HEAD_DIM), :]
            s = lax.dot_general(
                keys, qx[h, pl.ds(0, HEAD_DIM), :], cross, preferred_element_type=jnp.float32
            )
            s = s + bias_ref[...]
            peak = jnp.max(s, axis=0, keepdims=True)
            p = jnp.exp2(s - peak)
            m_s[h] = peak
            l_s[h] = jnp.sum(p, axis=0, keepdims=True)
            acc[h] = jnp.dot(
                kv[m, ch, pl.ds(fc + hh * HEAD_DIM, HEAD_DIM), :],
                p.astype(jnp.bfloat16),
                preferred_element_type=jnp.float32,
            )
        return carry

    lax.fori_loop(0, CHUNKS, own_chunk, 0)

    def tile(slot, ch):
        tags = kv[slot, ch, pl.ds(2 * fc, aug), :]
        for hh in range(hc):
            h = ch * hc + hh
            keys = jnp.concatenate([kv[slot, ch, pl.ds(hh * HEAD_DIM, HEAD_DIM), :], tags], axis=0)
            s = lax.dot_general(keys, qx[h], cross, preferred_element_type=jnp.float32)
            old = m_s[h]
            peak = jnp.maximum(old, jnp.max(s, axis=0, keepdims=True))
            rescale = jnp.exp2(old - peak)
            p = jnp.exp2(s - peak)
            m_s[h] = peak
            l_s[h] = l_s[h] * rescale + jnp.sum(p, axis=0, keepdims=True)
            acc[h] = acc[h] * rescale + jnp.dot(
                kv[slot, ch, pl.ds(fc + hh * HEAD_DIM, HEAD_DIM), :],
                p.astype(jnp.bfloat16),
                preferred_element_type=jnp.float32,
            )

    def step(g, carry):
        lev = g // CHUNKS
        ch = g % CHUNKS
        nxt = lev + 1
        a_on = (nxt <= reach) & (z - nxt >= 0)
        b_in = b_on(lev)
        c_in = cr_on(lev)

        @pl.when(a_on)
        def _():
            arrived(nxt * LEVEL + m, ch)
            send_column(nxt, ch)

        @pl.when(b_in)
        def _():
            arrived(lev * LEVEL + y_mem, ch)
            d_copy(lev, ch).start()

        @pl.when(a_on)
        def _():
            tile(nxt * LEVEL + m, ch)

        @pl.when(b_in)
        def _():
            tile(lev * LEVEL + y_mem, ch)

        @pl.when(c_in)
        def _():
            arrived(lev * LEVEL + core_mem, ch)
            tile(lev * LEVEL + core_mem, ch)

        @pl.when(b_in)
        def _():
            arrived(lev * LEVEL + diag_mem, ch)
            tile(lev * LEVEL + diag_mem, ch)

        return carry

    lax.fori_loop(0, (reach + 1) * CHUNKS, step, 0)

    for h in range(heads):
        flip[pl.ds(h * HEAD_DIM, HEAD_DIM), :] = (acc[h] / l_s[h]).astype(jnp.bfloat16)
    w_copy.wait()
    attn[...] = flip[...].T

    def p_copy(j, t):
        return pltpu.make_async_remote_copy(
            src_ref=sbuf.at[j - 1, t],
            dst_ref=rbuf.at[j - 1, t],
            send_sem=p_send.at[j - 1, t],
            recv_sem=p_recv.at[j - 1, t],
            device_id=(me, (me_tp + j) % tp),
            device_id_type=MESH,
        )

    def product(to, t):
        start = pl.multiple_of(to * feat + t * COLS, COLS)
        return jnp.dot(attn[...], w_s[:, pl.ds(start, COLS)], preferred_element_type=jnp.float32)

    for j in range(1, tp):

        def give(t, carry):
            sbuf[j - 1, t] = product((me_tp + j) % tp, t).astype(jnp.bfloat16)
            p_copy(j, t).start()
            return carry

        lax.fori_loop(0, nt, give, 0)

    def keep(t, carry):
        own_p[t] = product(me_tp, t)
        return carry

    lax.fori_loop(0, nt, keep, 0)

    square = jnp.zeros((tok, 1), jnp.float32)
    for t in range(nt):
        total = own_p[t]
        for j in range(1, tp):
            p_copy(j, t).wait_recv()
            total = total + rbuf[j - 1, t].astype(jnp.float32)
        cols = pl.ds(t * COLS, COLS)
        fresh = (hid_ref[:, cols].astype(jnp.float32) + total).astype(jnp.bfloat16)
        out_ref[:, cols] = fresh
        wide = fresh.astype(jnp.float32)
        square = square + jnp.sum(wide * wide, axis=1, keepdims=True)

    ssq_s[...] = jnp.broadcast_to(square, (tok, 128)).T[:8]

    def s_copy(j):
        return pltpu.make_async_remote_copy(
            src_ref=ssq_s,
            dst_ref=ssq_r.at[j - 1],
            send_sem=s_send.at[j - 1],
            recv_sem=s_recv.at[j - 1],
            device_id=(me, (me_tp + j) % tp),
            device_id_type=MESH,
        )

    for j in range(1, tp):
        s_copy(j).start()

    def drain(g, carry):
        lev = g // CHUNKS
        ch = g % CHUNKS

        @pl.when(z_on(lev))
        def _():
            z_copy(lev, ch).wait_send()

        @pl.when(y_on(lev))
        def _():
            y_copy(lev, ch).wait_send()

        @pl.when(c_on(lev))
        def _():
            c_copy(lev, ch).wait_send()

        @pl.when(b_on(lev))
        def _():
            d_copy(lev, ch).wait_send()

        return carry

    lax.fori_loop(0, (reach + 1) * CHUNKS, drain, 0)
    for j in range(1, tp):
        for t in range(nt):
            p_copy(j, t).wait_send()

    sums = ssq_s[...]
    for j in range(1, tp):
        s_copy(j).wait()
        sums = sums + ssq_r[j - 1]
    inverse = lax.rsqrt(sums / D + norm_epsilon)
    inverse = jnp.concatenate([inverse] * 16, axis=0).T[:, :1]
    for t in range(nt):
        cols = pl.ds(t * COLS, COLS)
        norm_ref[:, cols] = (
            out_ref[:, cols].astype(jnp.float32)
            * inverse
            * gain_ref[:, cols].astype(jnp.float32)
        ).astype(jnp.bfloat16)


def per_device(
    query_proj,
    key_proj,
    value_proj,
    hidden,
    out_weight,
    norm_gain,
    segment_ids,
    pad_mask,
    page_table,
):
    tok_count = query_proj.shape[0]
    feat_count = query_proj.shape[1]
    head_count = feat_count // HEAD_DIM
    seq = lax.axis_size("seq")
    tp = lax.axis_size("tp")
    seg_count = seq // 2
    reach = seq // (2 * LEVEL)
    device_row = lax.axis_index("seq")
    tok_index = device_row * tok_count + jnp.arange(tok_count, dtype=jnp.int32)
    member = segment_ids[:, None] == jnp.arange(seg_count, dtype=jnp.int32)[None, :]
    local_first = jnp.min(jnp.where(member, tok_index[:, None], far_index), axis=0)
    first_tok = lax.pmin(local_first, "seq")

    frequency = jnp.exp(
        jnp.arange(HALF, dtype=jnp.float32) * (-2.0 * math.log(10000.0) / HEAD_DIM)
    )
    angles = frequency[:, None] * tok_index.astype(jnp.float32)[None, :]
    cosine, sine = jnp.cos(angles), jnp.sin(angles)
    aug = max(16, seg_count)
    tags = jnp.where(pad_mask == 1, segment_ids, -1)
    slots = jnp.arange(aug, dtype=jnp.int32)[:, None]
    kaug = (slots != tags[None, :]).astype(jnp.bfloat16)
    qaug = jnp.where(slots == segment_ids[None, :], masked_score, 0.0).astype(jnp.bfloat16)
    offsets = jnp.arange(tok_count, dtype=jnp.int32)
    own_visible = (tags[:, None] == segment_ids[None, :]) & (
        offsets[:, None] <= offsets[None, :]
    ) | (offsets[:, None] == offsets[None, :])
    bias = jnp.where(own_visible, 0.0, masked_score).astype(jnp.float32)

    hc = head_count // CHUNKS
    fc = hc * HEAD_DIM
    nt = feat_count // COLS
    n_slots = (reach + 1) * LEVEL
    vm = pl.BlockSpec(memory_space=pltpu.VMEM)
    dma = pltpu.SemaphoreType.DMA
    flops = 4 * head_count * 9 * tok_count * tok_count * HEAD_DIM
    hidden_out, normed = pl.pallas_call(
        functools.partial(kernel, seq, tp),
        out_shape=[jax.ShapeDtypeStruct((tok_count, feat_count), jnp.bfloat16)] * 2,
        in_specs=[vm] * 10 + [pl.BlockSpec(memory_space=pl.ANY)],
        out_specs=[vm, vm],
        scratch_shapes=[
            pltpu.VMEM((n_slots, CHUNKS, 2 * fc + aug, tok_count), jnp.bfloat16),
            pltpu.VMEM((head_count, HEAD_DIM + aug, tok_count), jnp.bfloat16),
            pltpu.VMEM((feat_count, tok_count), jnp.bfloat16),
            pltpu.VMEM((tok_count, feat_count), jnp.bfloat16),
            pltpu.VMEM((head_count, 1, tok_count), jnp.float32),
            pltpu.VMEM((head_count, 1, tok_count), jnp.float32),
            pltpu.VMEM((head_count, HEAD_DIM, tok_count), jnp.float32),
            pltpu.VMEM(out_weight.shape, jnp.bfloat16),
            pltpu.VMEM((nt, tok_count, COLS), jnp.float32),
            pltpu.VMEM((tp - 1, nt, tok_count, COLS), jnp.bfloat16),
            pltpu.VMEM((tp - 1, nt, tok_count, COLS), jnp.bfloat16),
            pltpu.VMEM((8, tok_count), jnp.float32),
            pltpu.VMEM((tp - 1, 8, tok_count), jnp.float32),
            dma,
            dma((reach + 1, CHUNKS)),
            dma((reach + 1, CHUNKS)),
            dma((reach + 1, CHUNKS)),
            dma((reach + 1, CHUNKS)),
            dma((n_slots, CHUNKS)),
            dma((tp - 1, nt)),
            dma((tp - 1, nt)),
            dma((tp - 1,)),
            dma((tp - 1,)),
        ],
        compiler_params=pltpu.CompilerParams(
            collective_id=0, has_side_effects=True, vmem_limit_bytes=56 * 1024 * 1024
        ),
        cost_estimate=pl.CostEstimate(
            flops=flops, bytes_accessed=16 * 1024 * 1024, transcendentals=0
        ),
    )(
        query_proj,
        key_proj,
        value_proj,
        hidden,
        norm_gain[None, :],
        cosine,
        sine,
        kaug,
        qaug,
        bias,
        out_weight,
    )

    position = tok_index - jnp.sum(jnp.where(member, first_tok[None, :], 0), axis=1)
    k_rot = rotate(key_proj, position, head_count, HEAD_DIM)
    pad_scale = pad_mask.astype(jnp.bfloat16)[:, None]
    page_count = tok_count // PAGE
    stacked = jnp.stack([k_rot * pad_scale, value_proj * pad_scale])
    stacked = stacked.reshape(2, page_count, PAGE, feat_count).transpose(1, 0, 2, 3)
    kv_pages = jnp.zeros_like(stacked).at[page_table].set(stacked)
    return (hidden_out, normed, kv_pages)


def solution(mesh):
    placed = (
        P("seq", "tp"),
        P("seq", "tp"),
        P("seq", "tp"),
        P("seq", "tp"),
        P("tp", None),
        P("tp"),
        P("seq"),
        P("seq"),
        P("seq"),
    )
    return jax.shard_map(
        per_device,
        mesh=mesh,
        in_specs=placed,
        out_specs=(P("seq", "tp"), P("seq", "tp"), P("seq", None, None, "tp")),
        check_vma=False,
    )
```

```python
import functools
import math

import jax
import jax.numpy as jnp
from jax import lax
from jax.experimental import pallas as pl
from jax.experimental.pallas import tpu as pltpu
from jax.sharding import PartitionSpec as P

D = 3072
HEAD_DIM = 96
HALF = HEAD_DIM // 2
PAGE = 128
LEVEL = 4
CHUNK_MOST = 8
COLS = 384

far_index = 1073741824
masked_score = -1e30
norm_epsilon = 1e-05
MESH = pl.DeviceIdType.MESH


def kernel(
    seq,
    tp,
    q_ref,
    k_ref,
    v_ref,
    hid_ref,
    gain_ref,
    cos_ref,
    sin_ref,
    tags_ref,
    qaug_ref,
    bias_ref,
    place_ref,
    pad_ref,
    table_ref,
    w_hbm,
    out_ref,
    norm_ref,
    page_ref,
    kv,
    qx,
    flip,
    flip_k,
    tg,
    attn,
    m_s,
    l_s,
    acc,
    w_s,
    own_p,
    sbuf,
    rbuf,
    ssq_s,
    ssq_r,
    w_sem,
    z_send,
    y_send,
    c_send,
    d_send,
    recv,
    p_send,
    p_recv,
    s_send,
    s_recv,
    t_send,
    t_recv,
):
    tok, feat = q_ref.shape
    heads = feat // HEAD_DIM
    CHUNKS = min(CHUNK_MOST, heads)
    hc = heads // CHUNKS
    fc = hc * HEAD_DIM
    aug = qaug_ref.shape[0]
    reach = seq // (2 * LEVEL)
    nt = feat // COLS
    me = lax.axis_index("seq")
    me_tp = lax.axis_index("tp")
    z = me // LEVEL
    m = me % LEVEL
    my = m // 2
    mc = m % 2
    core_mem = my * 2 + (1 - mc)
    y_mem = (1 - my) * 2 + mc
    diag_mem = (1 - my) * 2 + (1 - mc)
    core_dev = z * LEVEL + core_mem
    y_dev = z * LEVEL + y_mem
    last_z = seq // LEVEL - 1
    span = reach * LEVEL

    w_copy = pltpu.make_async_copy(w_hbm, w_s, w_sem)
    w_copy.start()

    barrier = pltpu.get_barrier_semaphore()
    for j in range(1, tp):
        pl.semaphore_signal(
            barrier, inc=1, device_id=(me, (me_tp + j) % tp), device_id_type=MESH
        )
    for d in range(1, span + 1):

        @pl.when(me >= d)
        def _():
            pl.semaphore_signal(barrier, inc=1, device_id=(me - d, me_tp), device_id_type=MESH)

        @pl.when(me + d < seq)
        def _():
            pl.semaphore_signal(barrier, inc=1, device_id=(me + d, me_tp), device_id_type=MESH)

    flip[...] = v_ref[...].T
    for ch in range(CHUNKS):
        kv[m, ch, pl.ds(fc, fc), :] = flip[pl.ds(ch * fc, fc), :]
    flip_k[...] = k_ref[...].T

    pl.semaphore_wait(
        barrier, tp - 1 + jnp.minimum(me, span) + jnp.minimum(seq - 1 - me, span)
    )

    def t_copy(d):
        return pltpu.make_async_remote_copy(
            src_ref=tags_ref,
            dst_ref=tg.at[d - 1],
            send_sem=t_send.at[d - 1],
            recv_sem=t_recv.at[d - 1],
            device_id=(me + d, me_tp),
            device_id_type=MESH,
        )

    for d in range(1, span + 1):

        @pl.when(me + d < seq)
        def _():
            t_copy(d).start()

    def move(src_slot, dst_slot, ch, sem, dev):
        return pltpu.make_async_remote_copy(
            src_ref=kv.at[src_slot, ch],
            dst_ref=kv.at[dst_slot, ch],
            send_sem=sem,
            recv_sem=recv.at[dst_slot, ch],
            device_id=(dev, me_tp),
            device_id_type=MESH,
        )

    def z_copy(lev, ch):
        return move(lev * LEVEL + m, (lev + 1) * LEVEL + m, ch, z_send.at[lev, ch], me + LEVEL)

    def y_copy(lev, ch):
        slot = lev * LEVEL + m
        return move(slot, slot, ch, y_send.at[lev, ch], y_dev)

    def c_copy(lev, ch):
        slot = lev * LEVEL + m
        return move(slot, slot, ch, c_send.at[lev, ch], core_dev)

    def d_copy(lev, ch):
        slot = lev * LEVEL + y_mem
        return move(slot, slot, ch, d_send.at[lev, ch], core_dev)

    def arrived(slot, ch):
        pltpu.make_async_remote_copy(
            src_ref=kv.at[slot, ch],
            dst_ref=kv.at[slot, ch],
            send_sem=z_send.at[0, 0],
            recv_sem=recv.at[slot, ch],
            device_id=(core_dev, me_tp),
            device_id_type=MESH,
        ).wait_recv()

    def z_on(lev):
        return (z - lev >= 0) & (z < last_z) & (lev < reach)

    def band(lev, src, dst):
        return (z - lev >= 0) & ((lev > 0) | (src <= dst)) & ((lev < reach) | (src >= dst))

    def y_on(lev):
        return band(lev, my, 1 - my)

    def b_on(lev):
        return band(lev, 1 - my, my)

    def c_on(lev):
        return band(lev, mc, 1 - mc)

    def cr_on(lev):
        return band(lev, 1 - mc, mc)

    def send_column(lev, ch):
        @pl.when(z_on(lev))
        def _():
            z_copy(lev, ch).start()

        @pl.when(y_on(lev))
        def _():
            y_copy(lev, ch).start()

        @pl.when(c_on(lev))
        def _():
            c_copy(lev, ch).start()

    def turned(x, scale, cosine, sine):
        low = x[:HALF].astype(jnp.float32)
        high = x[HALF:].astype(jnp.float32)
        return (
            ((low * cosine - high * sine) * scale).astype(jnp.bfloat16),
            ((high * cosine + low * sine) * scale).astype(jnp.bfloat16),
        )

    for ch in range(CHUNKS):
        for hh in range(hc):
            first, second = turned(
                flip_k[pl.ds((ch * hc + hh) * HEAD_DIM, HEAD_DIM), :],
                1.0,
                cos_ref[...],
                sin_ref[...],
            )
            kv[m, ch, pl.ds(hh * HEAD_DIM, HALF), :] = first
            kv[m, ch, pl.ds(hh * HEAD_DIM + HALF, HALF), :] = second
        send_column(0, ch)

    flip[...] = q_ref[...].T
    for h in range(heads):
        first, second = turned(
            flip[pl.ds(h * HEAD_DIM, HEAD_DIM), :],
            math.log2(math.e) / math.sqrt(HEAD_DIM),
            cos_ref[...],
            sin_ref[...],
        )
        qx[h, pl.ds(0, HALF), :] = first
        qx[h, pl.ds(HALF, HALF), :] = second
        qx[h, pl.ds(HEAD_DIM, aug), :] = qaug_ref[...]

    cross = (((0,), (0,)), ((), ()))

    def own_chunk(ch, carry):
        for hh in range(hc):
            h = ch * hc + hh
            keys = kv[m, ch, pl.ds(hh * HEAD_DIM, HEAD_DIM), :]
            s = lax.dot_general(
                keys, qx[h, pl.ds(0, HEAD_DIM), :], cross, preferred_element_type=jnp.float32
            )
            s = s + bias_ref[...]
            peak = jnp.max(s, axis=0, keepdims=True)
            p = jnp.exp2(s - peak)
            m_s[h] = peak
            l_s[h] = jnp.sum(p, axis=0, keepdims=True)
            acc[h] = jnp.dot(
                kv[m, ch, pl.ds(fc + hh * HEAD_DIM, HEAD_DIM), :],
                p.astype(jnp.bfloat16),
                preferred_element_type=jnp.float32,
            )
        return carry

    lax.fori_loop(0, CHUNKS, own_chunk, 0)

    names = tags_ref[pl.ds(aug, 16), :][:1].astype(jnp.float32)
    opening = names[:, :1]
    count = jnp.zeros((1, tok), jnp.float32)
    for d in range(1, span + 1):

        @pl.when(me >= d)
        def _():
            t_copy(d).wait_recv()

        @pl.when(me < d)
        def _():
            tg[d - 1] = jnp.full(tg.shape[1:], -1.0, tg.dtype)

        earlier = tg[d - 1, pl.ds(aug, 16), :][:1].astype(jnp.float32)
        count = count + (earlier == opening).astype(jnp.float32)
    count = jnp.sum(count, axis=1, keepdims=True)
    place = place_ref[...] + jnp.where(names == opening, count, 0.0)
    rows = lax.broadcasted_iota(jnp.int32, (HALF, tok), 0).astype(jnp.float32)
    angles = jnp.exp(rows * (-2.0 * math.log(10000.0) / HEAD_DIM)) * place
    cosine = jnp.cos(angles)
    sine = jnp.sin(angles)
    for h in range(heads):
        first, second = turned(flip_k[pl.ds(h * HEAD_DIM, HEAD_DIM), :], 1.0, cosine, sine)
        flip[pl.ds(h * HEAD_DIM, HALF), :] = first
        flip[pl.ds(h * HEAD_DIM + HALF, HALF), :] = second
    attn[...] = flip[...].T
    in_order = table_ref[...][:1, :1] == 0.0
    for kind, ref in enumerate((attn, v_ref)):
        lower = ref[pl.ds(0, PAGE), :].astype(jnp.float32) * pad_ref[pl.ds(0, PAGE), :]
        upper = ref[pl.ds(PAGE, PAGE), :].astype(jnp.float32) * pad_ref[pl.ds(PAGE, PAGE), :]
        page_ref[0, kind] = jnp.where(in_order, lower, upper).astype(jnp.bfloat16)
        page_ref[1, kind] = jnp.where(in_order, upper, lower).astype(jnp.bfloat16)

    def tile(lev, mem, ch):
        slot = lev * LEVEL + mem
        tags = tg[lev * LEVEL + m - mem - 1, pl.ds(0, aug), :]
        for hh in range(hc):
            h = ch * hc + hh
            keys = jnp.concatenate([kv[slot, ch, pl.ds(hh * HEAD_DIM, HEAD_DIM), :], tags], axis=0)
            s = lax.dot_general(keys, qx[h], cross, preferred_element_type=jnp.float32)
            old = m_s[h]
            peak = jnp.maximum(old, jnp.max(s, axis=0, keepdims=True))
            rescale = jnp.exp2(old - peak)
            p = jnp.exp2(s - peak)
            m_s[h] = peak
            l_s[h] = l_s[h] * rescale + jnp.sum(p, axis=0, keepdims=True)
            acc[h] = acc[h] * rescale + jnp.dot(
                kv[slot, ch, pl.ds(fc + hh * HEAD_DIM, HEAD_DIM), :],
                p.astype(jnp.bfloat16),
                preferred_element_type=jnp.float32,
            )

    def step(g, carry):
        lev = g // CHUNKS
        ch = g % CHUNKS
        nxt = lev + 1
        a_on = (nxt <= reach) & (z - nxt >= 0)
        b_in = b_on(lev)
        c_in = cr_on(lev)

        @pl.when(a_on)
        def _():
            arrived(nxt * LEVEL + m, ch)
            send_column(nxt, ch)

        @pl.when(b_in)
        def _():
            arrived(lev * LEVEL + y_mem, ch)
            d_copy(lev, ch).start()

        @pl.when(a_on)
        def _():
            tile(nxt, m, ch)

        @pl.when(b_in)
        def _():
            tile(lev, y_mem, ch)

        @pl.when(c_in)
        def _():
            arrived(lev * LEVEL + core_mem, ch)
            tile(lev, core_mem, ch)

        @pl.when(b_in)
        def _():
            arrived(lev * LEVEL + diag_mem, ch)
            tile(lev, diag_mem, ch)

        return carry

    lax.fori_loop(0, (reach + 1) * CHUNKS, step, 0)

    for h in range(heads):
        flip[pl.ds(h * HEAD_DIM, HEAD_DIM), :] = (acc[h] / l_s[h]).astype(jnp.bfloat16)
    w_copy.wait()
    attn[...] = flip[...].T

    def p_copy(j, t):
        return pltpu.make_async_remote_copy(
            src_ref=sbuf.at[j - 1, t],
            dst_ref=rbuf.at[j - 1, t],
            send_sem=p_send.at[j - 1, t],
            recv_sem=p_recv.at[j - 1, t],
            device_id=(me, (me_tp + j) % tp),
            device_id_type=MESH,
        )

    def product(to, t):
        start = pl.multiple_of(to * feat + t * COLS, COLS)
        return jnp.dot(attn[...], w_s[:, pl.ds(start, COLS)], preferred_element_type=jnp.float32)

    for j in range(1, tp):

        def give(t, carry):
            sbuf[j - 1, t] = product((me_tp + j) % tp, t).astype(jnp.bfloat16)
            p_copy(j, t).start()
            return carry

        lax.fori_loop(0, nt, give, 0)

    def keep(t, carry):
        own_p[t] = product(me_tp, t)
        return carry

    lax.fori_loop(0, nt, keep, 0)

    square = jnp.zeros((tok, 1), jnp.float32)
    for t in range(nt):
        total = own_p[t]
        for j in range(1, tp):
            p_copy(j, t).wait_recv()
            total = total + rbuf[j - 1, t].astype(jnp.float32)
        cols = pl.ds(t * COLS, COLS)
        fresh = (hid_ref[:, cols].astype(jnp.float32) + total).astype(jnp.bfloat16)
        out_ref[:, cols] = fresh
        wide = fresh.astype(jnp.float32)
        square = square + jnp.sum(wide * wide, axis=1, keepdims=True)

    ssq_s[...] = jnp.broadcast_to(square, (tok, 128)).T[:8]

    def s_copy(j):
        return pltpu.make_async_remote_copy(
            src_ref=ssq_s,
            dst_ref=ssq_r.at[j - 1],
            send_sem=s_send.at[j - 1],
            recv_sem=s_recv.at[j - 1],
            device_id=(me, (me_tp + j) % tp),
            device_id_type=MESH,
        )

    for j in range(1, tp):
        s_copy(j).start()

    def drain(g, carry):
        lev = g // CHUNKS
        ch = g % CHUNKS

        @pl.when(z_on(lev))
        def _():
            z_copy(lev, ch).wait_send()

        @pl.when(y_on(lev))
        def _():
            y_copy(lev, ch).wait_send()

        @pl.when(c_on(lev))
        def _():
            c_copy(lev, ch).wait_send()

        @pl.when(b_on(lev))
        def _():
            d_copy(lev, ch).wait_send()

        return carry

    lax.fori_loop(0, (reach + 1) * CHUNKS, drain, 0)
    for j in range(1, tp):
        for t in range(nt):
            p_copy(j, t).wait_send()
    for d in range(1, span + 1):

        @pl.when(me + d < seq)
        def _():
            t_copy(d).wait_send()


    sums = ssq_s[...]
    for j in range(1, tp):
        s_copy(j).wait()
        sums = sums + ssq_r[j - 1]
    inverse = lax.rsqrt(sums / D + norm_epsilon)
    inverse = jnp.concatenate([inverse] * 16, axis=0).T[:, :1]
    for t in range(nt):
        cols = pl.ds(t * COLS, COLS)
        norm_ref[:, cols] = (
            out_ref[:, cols].astype(jnp.float32)
            * inverse
            * gain_ref[:, cols].astype(jnp.float32)
        ).astype(jnp.bfloat16)


def per_device(
    query_proj,
    key_proj,
    value_proj,
    hidden,
    out_weight,
    norm_gain,
    segment_ids,
    pad_mask,
    page_table,
):
    tok_count = query_proj.shape[0]
    feat_count = query_proj.shape[1]
    head_count = feat_count // HEAD_DIM
    seq = lax.axis_size("seq")
    tp = lax.axis_size("tp")
    seg_count = seq // 2
    reach = seq // (2 * LEVEL)
    device_row = lax.axis_index("seq")
    tok_index = device_row * tok_count + jnp.arange(tok_count, dtype=jnp.int32)
    member = segment_ids[:, None] == jnp.arange(seg_count, dtype=jnp.int32)[None, :]
    offsets = jnp.arange(tok_count, dtype=jnp.int32)
    local_first = jnp.min(jnp.where(member, offsets[:, None], far_index), axis=0)
    place = offsets - jnp.sum(jnp.where(member, local_first[None, :], 0), axis=1)

    frequency = jnp.exp(
        jnp.arange(HALF, dtype=jnp.float32) * (-2.0 * math.log(10000.0) / HEAD_DIM)
    )
    angles = frequency[:, None] * tok_index.astype(jnp.float32)[None, :]
    cosine, sine = jnp.cos(angles), jnp.sin(angles)
    aug = max(16, seg_count)
    tags = jnp.where(pad_mask == 1, segment_ids, -1)
    slots = jnp.arange(aug, dtype=jnp.int32)[:, None]
    carried = jnp.concatenate(
        [
            (slots != tags[None, :]).astype(jnp.bfloat16),
            jnp.broadcast_to(segment_ids.astype(jnp.bfloat16)[None, :], (16, tok_count)),
        ],
        axis=0,
    )
    qaug = jnp.where(slots == segment_ids[None, :], masked_score, 0.0).astype(jnp.bfloat16)
    own_visible = (tags[:, None] == segment_ids[None, :]) & (
        offsets[:, None] <= offsets[None, :]
    ) | (offsets[:, None] == offsets[None, :])
    bias = jnp.where(own_visible, 0.0, masked_score).astype(jnp.float32)

    CHUNKS = min(CHUNK_MOST, head_count)
    hc = head_count // CHUNKS
    fc = hc * HEAD_DIM
    nt = feat_count // COLS
    n_slots = (reach + 1) * LEVEL
    vm = pl.BlockSpec(memory_space=pltpu.VMEM)
    dma = pltpu.SemaphoreType.DMA
    flops = 4 * head_count * 9 * tok_count * tok_count * HEAD_DIM
    return pl.pallas_call(
        functools.partial(kernel, seq, tp),
        out_shape=[jax.ShapeDtypeStruct((tok_count, feat_count), jnp.bfloat16)] * 2
        + [jax.ShapeDtypeStruct((tok_count // PAGE, 2, PAGE, feat_count), jnp.bfloat16)],
        in_specs=[vm] * 13 + [pl.BlockSpec(memory_space=pl.ANY)],
        out_specs=[vm, vm, vm],
        scratch_shapes=[
            pltpu.VMEM((n_slots, CHUNKS, 2 * fc, tok_count), jnp.bfloat16),
            pltpu.VMEM((head_count, HEAD_DIM + aug, tok_count), jnp.bfloat16),
            pltpu.VMEM((feat_count, tok_count), jnp.bfloat16),
            pltpu.VMEM((feat_count, tok_count), jnp.bfloat16),
            pltpu.VMEM((reach * LEVEL, aug + 16, tok_count), jnp.bfloat16),
            pltpu.VMEM((tok_count, feat_count), jnp.bfloat16),
            pltpu.VMEM((head_count, 1, tok_count), jnp.float32),
            pltpu.VMEM((head_count, 1, tok_count), jnp.float32),
            pltpu.VMEM((head_count, HEAD_DIM, tok_count), jnp.float32),
            pltpu.VMEM(out_weight.shape, jnp.bfloat16),
            pltpu.VMEM((nt, tok_count, COLS), jnp.float32),
            pltpu.VMEM((tp - 1, nt, tok_count, COLS), jnp.bfloat16),
            pltpu.VMEM((tp - 1, nt, tok_count, COLS), jnp.bfloat16),
            pltpu.VMEM((8, tok_count), jnp.float32),
            pltpu.VMEM((tp - 1, 8, tok_count), jnp.float32),
            dma,
            dma((reach + 1, CHUNKS)),
            dma((reach + 1, CHUNKS)),
            dma((reach + 1, CHUNKS)),
            dma((reach + 1, CHUNKS)),
            dma((n_slots, CHUNKS)),
            dma((tp - 1, nt)),
            dma((tp - 1, nt)),
            dma((tp - 1,)),
            dma((tp - 1,)),
            dma((reach * LEVEL,)),
            dma((reach * LEVEL,)),
        ],
        compiler_params=pltpu.CompilerParams(
            collective_id=0, has_side_effects=True, vmem_limit_bytes=56 * 1024 * 1024
        ),
        cost_estimate=pl.CostEstimate(
            flops=flops, bytes_accessed=16 * 1024 * 1024, transcendentals=0
        ),
    )(
        query_proj,
        key_proj,
        value_proj,
        hidden,
        norm_gain[None, :],
        cosine,
        sine,
        carried,
        qaug,
        bias,
        place.astype(jnp.float32)[None, :],
        pad_mask.astype(jnp.float32)[:, None],
        jnp.broadcast_to(page_table[:1].astype(jnp.float32)[None, :], (8, 128)),
        out_weight,
    )


def solution(mesh):
    placed = (
        P("seq", "tp"),
        P("seq", "tp"),
        P("seq", "tp"),
        P("seq", "tp"),
        P("tp", None),
        P("tp"),
        P("seq"),
        P("seq"),
        P("seq"),
    )
    return jax.shard_map(
        per_device,
        mesh=mesh,
        in_specs=placed,
        out_specs=(P("seq", "tp"), P("seq", "tp"), P("seq", None, None, "tp")),
        check_vma=False,
    )
```

```python
import functools
import math

import jax
import jax.numpy as jnp
from jax import lax
from jax.experimental import pallas as pl
from jax.experimental.pallas import tpu as pltpu
from jax.sharding import PartitionSpec as P

D = 3072
HEAD_DIM = 96
HALF = HEAD_DIM // 2
PAGE = 128
LEVEL = 4
CHUNK_MOST = 8
LAG = 2
COLS = 384

far_index = 1073741824
masked_score = -1e30
norm_epsilon = 1e-05
MESH = pl.DeviceIdType.MESH


def kernel(
    seq,
    tp,
    q_ref,
    k_ref,
    v_ref,
    hid_ref,
    gain_ref,
    cos_ref,
    sin_ref,
    tags_ref,
    qaug_ref,
    bias_ref,
    place_ref,
    pad_ref,
    table_ref,
    w_hbm,
    out_ref,
    norm_ref,
    page_ref,
    kv,
    qx,
    flip,
    flip_k,
    tg,
    attn,
    m_s,
    l_s,
    acc,
    w_s,
    own_p,
    w_far,
    a_far,
    ssq_s,
    ssq_r,
    w_sem,
    z_send,
    y_send,
    c_send,
    d_send,
    recv,
    a_send,
    a_recv,
    wf_send,
    wf_recv,
    wc_send,
    wc_recv,
    s_send,
    s_recv,
    t_send,
    t_recv,
):
    tok, feat = q_ref.shape
    heads = feat // HEAD_DIM
    CHUNKS = min(CHUNK_MOST, heads)
    hc = heads // CHUNKS
    fc = hc * HEAD_DIM
    aug = qaug_ref.shape[0]
    reach = seq // (2 * LEVEL)
    nt = feat // COLS
    me = lax.axis_index("seq")
    me_tp = lax.axis_index("tp")
    z = me // LEVEL
    m = me % LEVEL
    my = m // 2
    mc = m % 2
    core_mem = my * 2 + (1 - mc)
    y_mem = (1 - my) * 2 + mc
    diag_mem = (1 - my) * 2 + (1 - mc)
    core_dev = z * LEVEL + core_mem
    y_dev = z * LEVEL + y_mem
    last_z = seq // LEVEL - 1
    span = reach * LEVEL

    w_copy = pltpu.make_async_copy(
        w_hbm.at[:, pl.ds(pl.multiple_of(me_tp * feat, 128), feat)], w_s, w_sem
    )
    w_copy.start()
    half = feat // 2

    barrier = pltpu.get_barrier_semaphore()
    for j in range(1, tp):
        pl.semaphore_signal(
            barrier, inc=1, device_id=(me, (me_tp + j) % tp), device_id_type=MESH
        )
    for d in range(1, span + 1):

        @pl.when(me >= d)
        def _():
            pl.semaphore_signal(barrier, inc=1, device_id=(me - d, me_tp), device_id_type=MESH)

        @pl.when(me + d < seq)
        def _():
            pl.semaphore_signal(barrier, inc=1, device_id=(me + d, me_tp), device_id_type=MESH)

    flip[...] = v_ref[...].T
    for ch in range(CHUNKS):
        kv[m, ch, pl.ds(fc, fc), :] = flip[pl.ds(ch * fc, fc), :]
    flip_k[...] = k_ref[...].T

    pl.semaphore_wait(
        barrier, tp - 1 + jnp.minimum(me, span) + jnp.minimum(seq - 1 - me, span)
    )

    def t_copy(d):
        return pltpu.make_async_remote_copy(
            src_ref=tags_ref,
            dst_ref=tg.at[d - 1],
            send_sem=t_send.at[d - 1],
            recv_sem=t_recv.at[d - 1],
            device_id=(me + d, me_tp),
            device_id_type=MESH,
        )

    for d in range(1, span + 1):

        @pl.when(me + d < seq)
        def _():
            t_copy(d).start()

    def w_copy_far(j):
        to = (me_tp + j) % tp
        rows = pl.ds(pl.multiple_of(mc * half, 16), half)
        return pltpu.make_async_remote_copy(
            src_ref=w_hbm.at[rows, pl.ds(pl.multiple_of(to * feat, 128), feat)],
            dst_ref=w_far.at[j - 1, rows, :],
            send_sem=wf_send.at[j - 1],
            recv_sem=wf_recv.at[j - 1],
            device_id=(me, to),
            device_id_type=MESH,
        )

    def w_between(j, core):
        rows = pl.ds(pl.multiple_of(core * half, 16), half)
        return pltpu.make_async_remote_copy(
            src_ref=w_far.at[j - 1, rows, :],
            dst_ref=w_far.at[j - 1, rows, :],
            send_sem=wc_send.at[j - 1],
            recv_sem=wc_recv.at[j - 1],
            device_id=(core_dev, me_tp),
            device_id_type=MESH,
        )

    def w_copy_core(j):
        return w_between(j, mc)

    def w_core_arrived(j):
        w_between(j, 1 - mc).wait_recv()

    def a_copy(j, ch):
        rows = pl.ds(pl.multiple_of(ch * fc, 16), fc)
        return pltpu.make_async_remote_copy(
            src_ref=flip.at[rows, :],
            dst_ref=a_far.at[j - 1, rows, :],
            send_sem=a_send.at[j - 1, ch],
            recv_sem=a_recv.at[j - 1, ch],
            device_id=(me, (me_tp + j) % tp),
            device_id_type=MESH,
        )

    def move(src_slot, dst_slot, ch, sem, dev):
        return pltpu.make_async_remote_copy(
            src_ref=kv.at[src_slot, ch],
            dst_ref=kv.at[dst_slot, ch],
            send_sem=sem,
            recv_sem=recv.at[dst_slot, ch],
            device_id=(dev, me_tp),
            device_id_type=MESH,
        )

    def z_copy(lev, ch):
        return move(lev * LEVEL + m, (lev + 1) * LEVEL + m, ch, z_send.at[lev, ch], me + LEVEL)

    def y_copy(lev, ch):
        slot = lev * LEVEL + m
        return move(slot, slot, ch, y_send.at[lev, ch], y_dev)

    def c_copy(lev, ch):
        slot = lev * LEVEL + m
        return move(slot, slot, ch, c_send.at[lev, ch], core_dev)

    def d_copy(lev, ch):
        slot = lev * LEVEL + y_mem
        return move(slot, slot, ch, d_send.at[lev, ch], core_dev)

    def arrived(slot, ch):
        pltpu.make_async_remote_copy(
            src_ref=kv.at[slot, ch],
            dst_ref=kv.at[slot, ch],
            send_sem=z_send.at[0, 0],
            recv_sem=recv.at[slot, ch],
            device_id=(core_dev, me_tp),
            device_id_type=MESH,
        ).wait_recv()

    def z_on(lev):
        return (z - lev >= 0) & (z < last_z) & (lev < reach)

    def band(lev, src, dst):
        return (z - lev >= 0) & ((lev > 0) | (src <= dst)) & ((lev < reach) | (src >= dst))

    def y_on(lev):
        return band(lev, my, 1 - my)

    def b_on(lev):
        return band(lev, 1 - my, my)

    def c_on(lev):
        return band(lev, mc, 1 - mc)

    def cr_on(lev):
        return band(lev, 1 - mc, mc)

    def send_column(lev, ch):
        @pl.when(z_on(lev))
        def _():
            z_copy(lev, ch).start()

        @pl.when(y_on(lev))
        def _():
            y_copy(lev, ch).start()

        @pl.when(c_on(lev))
        def _():
            c_copy(lev, ch).start()

    def turned(x, scale, cosine, sine):
        low = x[:HALF].astype(jnp.float32)
        high = x[HALF:].astype(jnp.float32)
        return (
            ((low * cosine - high * sine) * scale).astype(jnp.bfloat16),
            ((high * cosine + low * sine) * scale).astype(jnp.bfloat16),
        )

    for ch in range(CHUNKS):
        for hh in range(hc):
            first, second = turned(
                flip_k[pl.ds((ch * hc + hh) * HEAD_DIM, HEAD_DIM), :],
                1.0,
                cos_ref[...],
                sin_ref[...],
            )
            kv[m, ch, pl.ds(hh * HEAD_DIM, HALF), :] = first
            kv[m, ch, pl.ds(hh * HEAD_DIM + HALF, HALF), :] = second
        send_column(0, ch)
    for j in range(1, tp):
        w_copy_far(j).start()

    flip[...] = q_ref[...].T
    for h in range(heads):
        first, second = turned(
            flip[pl.ds(h * HEAD_DIM, HEAD_DIM), :],
            math.log2(math.e) / math.sqrt(HEAD_DIM),
            cos_ref[...],
            sin_ref[...],
        )
        qx[h, pl.ds(0, HALF), :] = first
        qx[h, pl.ds(HALF, HALF), :] = second
        qx[h, pl.ds(HEAD_DIM, aug), :] = qaug_ref[...]

    cross = (((0,), (0,)), ((), ()))

    def own_chunk(ch, carry):
        for hh in range(hc):
            h = ch * hc + hh
            keys = kv[m, ch, pl.ds(hh * HEAD_DIM, HEAD_DIM), :]
            s = lax.dot_general(
                keys, qx[h, pl.ds(0, HEAD_DIM), :], cross, preferred_element_type=jnp.float32
            )
            s = s + bias_ref[...]
            peak = jnp.max(s, axis=0, keepdims=True)
            p = jnp.exp2(s - peak)
            m_s[h] = peak
            l_s[h] = jnp.sum(p, axis=0, keepdims=True)
            acc[h] = jnp.dot(
                kv[m, ch, pl.ds(fc + hh * HEAD_DIM, HEAD_DIM), :],
                p.astype(jnp.bfloat16),
                preferred_element_type=jnp.float32,
            )
        return carry

    lax.fori_loop(0, CHUNKS, own_chunk, 0)

    names = tags_ref[pl.ds(aug, 16), :][:1].astype(jnp.float32)
    opening = names[:, :1]
    count = jnp.zeros((1, tok), jnp.float32)
    for d in range(1, span + 1):

        @pl.when(me >= d)
        def _():
            t_copy(d).wait_recv()

        @pl.when(me < d)
        def _():
            tg[d - 1] = jnp.full(tg.shape[1:], -1.0, tg.dtype)

        earlier = tg[d - 1, pl.ds(aug, 16), :][:1].astype(jnp.float32)
        count = count + (earlier == opening).astype(jnp.float32)
    count = jnp.sum(count, axis=1, keepdims=True)
    place = place_ref[...] + jnp.where(names == opening, count, 0.0)
    rows = lax.broadcasted_iota(jnp.int32, (HALF, tok), 0).astype(jnp.float32)
    angles = jnp.exp(rows * (-2.0 * math.log(10000.0) / HEAD_DIM)) * place
    cosine = jnp.cos(angles)
    sine = jnp.sin(angles)
    for h in range(heads):
        first, second = turned(flip_k[pl.ds(h * HEAD_DIM, HEAD_DIM), :], 1.0, cosine, sine)
        flip[pl.ds(h * HEAD_DIM, HALF), :] = first
        flip[pl.ds(h * HEAD_DIM + HALF, HALF), :] = second
    attn[...] = flip[...].T
    in_order = table_ref[...][:1, :1] == 0.0
    for kind, ref in enumerate((attn, v_ref)):
        lower = ref[pl.ds(0, PAGE), :].astype(jnp.float32) * pad_ref[pl.ds(0, PAGE), :]
        upper = ref[pl.ds(PAGE, PAGE), :].astype(jnp.float32) * pad_ref[pl.ds(PAGE, PAGE), :]
        page_ref[0, kind] = jnp.where(in_order, lower, upper).astype(jnp.bfloat16)
        page_ref[1, kind] = jnp.where(in_order, upper, lower).astype(jnp.bfloat16)

    def tile(lev, mem, ch):
        slot = lev * LEVEL + mem
        tags = tg[lev * LEVEL + m - mem - 1, pl.ds(0, aug), :]
        for hh in range(hc):
            h = ch * hc + hh
            keys = jnp.concatenate([kv[slot, ch, pl.ds(hh * HEAD_DIM, HEAD_DIM), :], tags], axis=0)
            s = lax.dot_general(keys, qx[h], cross, preferred_element_type=jnp.float32)
            old = m_s[h]
            peak = jnp.maximum(old, jnp.max(s, axis=0, keepdims=True))
            rescale = jnp.exp2(old - peak)
            p = jnp.exp2(s - peak)
            m_s[h] = peak
            l_s[h] = l_s[h] * rescale + jnp.sum(p, axis=0, keepdims=True)
            acc[h] = acc[h] * rescale + jnp.dot(
                kv[slot, ch, pl.ds(fc + hh * HEAD_DIM, HEAD_DIM), :],
                p.astype(jnp.bfloat16),
                preferred_element_type=jnp.float32,
            )

    def others(lev, ch):
        b_in = b_on(lev)

        @pl.when(b_in)
        def _():
            arrived(lev * LEVEL + y_mem, ch)
            d_copy(lev, ch).start()
            tile(lev, y_mem, ch)

        @pl.when(cr_on(lev))
        def _():
            arrived(lev * LEVEL + core_mem, ch)
            tile(lev, core_mem, ch)

        @pl.when(b_in)
        def _():
            arrived(lev * LEVEL + diag_mem, ch)
            tile(lev, diag_mem, ch)

    def finish(ch):
        for hh in range(hc):
            h = ch * hc + hh
            rows = pl.ds(pl.multiple_of(h * HEAD_DIM, HEAD_DIM), HEAD_DIM)
            flip[rows, :] = (acc[h] / l_s[h]).astype(jnp.bfloat16)
        for j in range(1, tp):
            a_copy(j, ch).start()

    late = (reach - 1) * CHUNKS + LAG

    def step(g, carry):
        lev = g // CHUNKS
        ch = g % CHUNKS
        nxt = lev + 1
        a_on = (nxt <= reach) & (z - nxt >= 0)

        @pl.when(a_on)
        def _():
            arrived(nxt * LEVEL + m, ch)
            send_column(nxt, ch)
            tile(nxt, m, ch)

        @pl.when(lev < reach)
        def _():
            others(lev, ch)

        @pl.when(g >= late)
        def _():
            others(reach, g - late)
            finish(g - late)

        @pl.when(g == reach * CHUNKS - 1)
        def _():
            for j in range(1, tp):
                w_copy_far(j).wait_recv()
                w_copy_core(j).start()

        return carry

    lax.fori_loop(0, reach * CHUNKS + LAG, step, 0)

    w_copy.wait()
    attn[...] = flip[...].T

    def keep(t, carry):
        cols = pl.ds(pl.multiple_of(t * COLS, COLS), COLS)
        own_p[t] = jnp.dot(attn[...], w_s[:, cols], preferred_element_type=jnp.float32)
        return carry

    lax.fori_loop(0, nt, keep, 0)
    for j in range(1, tp):
        for ch in range(CHUNKS):
            a_copy(j, ch).wait_recv()
        w_core_arrived(j)
        attn[...] = a_far[j - 1].T

        def more(t, carry):
            cols = pl.ds(pl.multiple_of(t * COLS, COLS), COLS)
            own_p[t] = own_p[t] + jnp.dot(
                attn[...], w_far[j - 1, :, cols], preferred_element_type=jnp.float32
            )
            return carry

        lax.fori_loop(0, nt, more, 0)

    square = jnp.zeros((tok, 1), jnp.float32)
    for t in range(nt):
        total = own_p[t]
        cols = pl.ds(t * COLS, COLS)
        fresh = (hid_ref[:, cols].astype(jnp.float32) + total).astype(jnp.bfloat16)
        out_ref[:, cols] = fresh
        wide = fresh.astype(jnp.float32)
        square = square + jnp.sum(wide * wide, axis=1, keepdims=True)

    ssq_s[...] = jnp.broadcast_to(square, (tok, 128)).T[:8]

    def s_copy(j):
        return pltpu.make_async_remote_copy(
            src_ref=ssq_s,
            dst_ref=ssq_r.at[j - 1],
            send_sem=s_send.at[j - 1],
            recv_sem=s_recv.at[j - 1],
            device_id=(me, (me_tp + j) % tp),
            device_id_type=MESH,
        )

    for j in range(1, tp):
        s_copy(j).start()

    def drain(g, carry):
        lev = g // CHUNKS
        ch = g % CHUNKS

        @pl.when(z_on(lev))
        def _():
            z_copy(lev, ch).wait_send()

        @pl.when(y_on(lev))
        def _():
            y_copy(lev, ch).wait_send()

        @pl.when(c_on(lev))
        def _():
            c_copy(lev, ch).wait_send()

        @pl.when(b_on(lev))
        def _():
            d_copy(lev, ch).wait_send()

        return carry

    lax.fori_loop(0, (reach + 1) * CHUNKS, drain, 0)
    for j in range(1, tp):
        for ch in range(CHUNKS):
            a_copy(j, ch).wait_send()
        w_copy_far(j).wait_send()
        w_copy_core(j).wait_send()
    for d in range(1, span + 1):

        @pl.when(me + d < seq)
        def _():
            t_copy(d).wait_send()


    sums = ssq_s[...]
    for j in range(1, tp):
        s_copy(j).wait()
        sums = sums + ssq_r[j - 1]
    inverse = lax.rsqrt(sums / D + norm_epsilon)
    inverse = jnp.concatenate([inverse] * 16, axis=0).T[:, :1]
    for t in range(nt):
        cols = pl.ds(t * COLS, COLS)
        norm_ref[:, cols] = (
            out_ref[:, cols].astype(jnp.float32)
            * inverse
            * gain_ref[:, cols].astype(jnp.float32)
        ).astype(jnp.bfloat16)


def per_device(
    query_proj,
    key_proj,
    value_proj,
    hidden,
    out_weight,
    norm_gain,
    segment_ids,
    pad_mask,
    page_table,
):
    tok_count = query_proj.shape[0]
    feat_count = query_proj.shape[1]
    head_count = feat_count // HEAD_DIM
    seq = lax.axis_size("seq")
    tp = lax.axis_size("tp")
    seg_count = seq // 2
    reach = seq // (2 * LEVEL)
    device_row = lax.axis_index("seq")
    tok_index = device_row * tok_count + jnp.arange(tok_count, dtype=jnp.int32)
    member = segment_ids[:, None] == jnp.arange(seg_count, dtype=jnp.int32)[None, :]
    offsets = jnp.arange(tok_count, dtype=jnp.int32)
    local_first = jnp.min(jnp.where(member, offsets[:, None], far_index), axis=0)
    place = offsets - jnp.sum(jnp.where(member, local_first[None, :], 0), axis=1)

    frequency = jnp.exp(
        jnp.arange(HALF, dtype=jnp.float32) * (-2.0 * math.log(10000.0) / HEAD_DIM)
    )
    angles = frequency[:, None] * tok_index.astype(jnp.float32)[None, :]
    cosine, sine = jnp.cos(angles), jnp.sin(angles)
    aug = max(16, seg_count)
    tags = jnp.where(pad_mask == 1, segment_ids, -1)
    slots = jnp.arange(aug, dtype=jnp.int32)[:, None]
    carried = jnp.concatenate(
        [
            (slots != tags[None, :]).astype(jnp.bfloat16),
            jnp.broadcast_to(segment_ids.astype(jnp.bfloat16)[None, :], (16, tok_count)),
        ],
        axis=0,
    )
    qaug = jnp.where(slots == segment_ids[None, :], masked_score, 0.0).astype(jnp.bfloat16)
    own_visible = (tags[:, None] == segment_ids[None, :]) & (
        offsets[:, None] <= offsets[None, :]
    ) | (offsets[:, None] == offsets[None, :])
    bias = jnp.where(own_visible, 0.0, masked_score).astype(jnp.float32)

    CHUNKS = min(CHUNK_MOST, head_count)
    hc = head_count // CHUNKS
    fc = hc * HEAD_DIM
    nt = feat_count // COLS
    n_slots = (reach + 1) * LEVEL
    vm = pl.BlockSpec(memory_space=pltpu.VMEM)
    dma = pltpu.SemaphoreType.DMA
    flops = 4 * head_count * 9 * tok_count * tok_count * HEAD_DIM
    return pl.pallas_call(
        functools.partial(kernel, seq, tp),
        out_shape=[jax.ShapeDtypeStruct((tok_count, feat_count), jnp.bfloat16)] * 2
        + [jax.ShapeDtypeStruct((tok_count // PAGE, 2, PAGE, feat_count), jnp.bfloat16)],
        in_specs=[vm] * 13 + [pl.BlockSpec(memory_space=pl.ANY)],
        out_specs=[vm, vm, vm],
        scratch_shapes=[
            pltpu.VMEM((n_slots, CHUNKS, 2 * fc, tok_count), jnp.bfloat16),
            pltpu.VMEM((head_count, HEAD_DIM + aug, tok_count), jnp.bfloat16),
            pltpu.VMEM((feat_count, tok_count), jnp.bfloat16),
            pltpu.VMEM((feat_count, tok_count), jnp.bfloat16),
            pltpu.VMEM((reach * LEVEL, aug + 16, tok_count), jnp.bfloat16),
            pltpu.VMEM((tok_count, feat_count), jnp.bfloat16),
            pltpu.VMEM((head_count, 1, tok_count), jnp.float32),
            pltpu.VMEM((head_count, 1, tok_count), jnp.float32),
            pltpu.VMEM((head_count, HEAD_DIM, tok_count), jnp.float32),
            pltpu.VMEM((feat_count, feat_count), jnp.bfloat16),
            pltpu.VMEM((nt, tok_count, COLS), jnp.float32),
            pltpu.VMEM((tp - 1, feat_count, feat_count), jnp.bfloat16),
            pltpu.VMEM((tp - 1, feat_count, tok_count), jnp.bfloat16),
            pltpu.VMEM((8, tok_count), jnp.float32),
            pltpu.VMEM((tp - 1, 8, tok_count), jnp.float32),
            dma,
            dma((reach + 1, CHUNKS)),
            dma((reach + 1, CHUNKS)),
            dma((reach + 1, CHUNKS)),
            dma((reach + 1, CHUNKS)),
            dma((n_slots, CHUNKS)),
            dma((tp - 1, CHUNKS)),
            dma((tp - 1, CHUNKS)),
            dma((tp - 1,)),
            dma((tp - 1,)),
            dma((tp - 1,)),
            dma((tp - 1,)),
            dma((tp - 1,)),
            dma((tp - 1,)),
            dma((reach * LEVEL,)),
            dma((reach * LEVEL,)),
        ],
        compiler_params=pltpu.CompilerParams(
            collective_id=0, has_side_effects=True, vmem_limit_bytes=56 * 1024 * 1024
        ),
        cost_estimate=pl.CostEstimate(
            flops=flops, bytes_accessed=16 * 1024 * 1024, transcendentals=0
        ),
    )(
        query_proj,
        key_proj,
        value_proj,
        hidden,
        norm_gain[None, :],
        cosine,
        sine,
        carried,
        qaug,
        bias,
        place.astype(jnp.float32)[None, :],
        pad_mask.astype(jnp.float32)[:, None],
        jnp.broadcast_to(page_table[:1].astype(jnp.float32)[None, :], (8, 128)),
        out_weight,
    )


def solution(mesh):
    placed = (
        P("seq", "tp"),
        P("seq", "tp"),
        P("seq", "tp"),
        P("seq", "tp"),
        P("tp", None),
        P("tp"),
        P("seq"),
        P("seq"),
        P("seq"),
    )
    return jax.shard_map(
        per_device,
        mesh=mesh,
        in_specs=placed,
        out_specs=(P("seq", "tp"), P("seq", "tp"), P("seq", None, None, "tp")),
        check_vma=False,
    )
```
